32 devices in a mesh: dp: 16 (over z, y, core), tensor: 2 (over x).
Axes of the slice: x: 2, y: 2, z: 4, core: 2. Of those that a mesh axis runs over, the one named last changes fastest.
Arguments:
- hidden: bfloat16 [16384, 768], P(('dp', 'tensor')), may hold values from -6 to 6
- segments: int32 [16, 1024], P('dp'), may hold values from 0 to 3, as said below
- norm_gain: float32 [768], replicated, may hold values from 0.5 to 1.5
- proj_gate: bfloat16 [768, 1536], P('dp', 'tensor'), may hold values from -0.21875 to 0.21875
- proj_value: bfloat16 [768, 1536], P('dp', 'tensor'), may hold values from -0.21875 to 0.21875
- proj_bc: bfloat16 [768, 256], P(('dp', 'tensor')), may hold values from -0.21875 to 0.21875
- proj_step: bfloat16 [768, 24], P('dp', 'tensor'), may hold values from -0.21875 to 0.21875
- conv_value: float32 [4, 1536], P(None, 'tensor'), may hold values from -3 to 3
- conv_bc: float32 [4, 256], replicated, may hold values from -3 to 3
- conv_value_bias: float32 [1536], P('tensor'), may hold values from -3 to 3
- conv_bc_bias: float32 [256], replicated, may hold values from -3 to 3
- step_bias: float32 [24], P('tensor'), may hold values from -5 to -1
- decay_log: float32 [24], P('tensor'), may hold values from -3 to 1
- skip_gain: float32 [24], P('tensor'), may hold values from 0 to 2
- gate_gain: float32 [1536], P('tensor'), may hold values from 0.5 to 1.5
- out_weight: bfloat16 [768, 1536], P('dp', 'tensor'), may hold values from -0.15625 to 0.15625
- cotangent: bfloat16 [16384, 768], P(('dp', 'tensor')), may hold values from -6 to 6
Outputs:
- mixed: bfloat16 [16384, 768], P(('dp', 'tensor'))
- grad_hidden: float32 [16384, 768], P(('dp', 'tensor'))
- grad_norm_gain: float32 [768], replicated
- grad_proj_gate: float32 [768, 1536], P('dp', 'tensor')
- grad_proj_value: float32 [768, 1536], P('dp', 'tensor')
- grad_proj_bc: float32 [768, 256], P(('dp', 'tensor'))
- grad_proj_step: float32 [768, 24], P('dp', 'tensor')
- grad_conv_value: float32 [4, 1536], P(None, 'tensor')
- grad_conv_bc: float32 [4, 256], replicated
- grad_conv_value_bias: float32 [1536], P('tensor')
- grad_conv_bc_bias: float32 [256], replicated
- grad_step_bias: float32 [24], P('tensor')
- grad_decay_log: float32 [24], P('tensor')
- grad_skip_gain: float32 [24], P('tensor')
- grad_gate_gain: float32 [1536], P('tensor')
- grad_out_weight: float32 [768, 1536], P('dp', 'tensor')
The draws below stay inside these ranges and needn't reach their ends.
Inputs may be any that keep to these rules, and one draw needn't show every extreme that they name: `segments`: within each packed sequence the numbers start at 0 and rise by one at each document start, so every sequence holds four documents, and one of them holds both token 511 and token 512.
All inputs are finite; a program needn't handle non-finite values.
Results may differ from the reference program's by a relative error of at most 0.0087.
Values may be sent and summed in bfloat16 or wider, within the bound.
A program may use at most 192 MiB of HBM per device.

```python
import math
import jax
import jax.numpy as jnp
from jax import lax

D = 768
H = 24
N = 128
K = 4
GROUP = 256
LEN = 1024
DI = 1536
NSEQ = 16
TOKENS = 16384


def draw_segments(key, part):
    key = jax.random.fold_in(key, 11)
    subkeys = jax.random.split(key, 3)
    quarter = max(LEN // 4, 2)
    smallest = max(LEN // 64, 1)
    first_cut = jax.random.randint(subkeys[0], (NSEQ, 1), smallest, quarter)
    second_cut = first_cut + jax.random.randint(subkeys[1], (NSEQ, 1), smallest, quarter)
    third_cut = jax.random.randint(subkeys[2], (NSEQ, 1), LEN // 2 + max(LEN // 16, 1), LEN - smallest)
    position = jnp.arange(LEN, dtype=jnp.int32)[None, :]
    counted = (position >= first_cut).astype(jnp.int32) + (position >= second_cut).astype(jnp.int32) + (position >= third_cut).astype(jnp.int32)
    return counted.astype(jnp.int32)


def shard_levels(own_key, extent, cuts, low, high):
    def one(dim, blocks):
        heights = jax.random.uniform(jax.random.fold_in(jax.random.fold_in(own_key, 6), dim), (blocks,), jnp.float32, low / len(cuts), high / len(cuts))
        return jnp.repeat(jnp.exp(heights), extent[dim] // blocks).reshape((-1,) + (1,) * (len(extent) - dim - 1))

    level = one(*cuts[0])
    for cut in cuts[1:]:
        level = level * one(*cut)
    return level


def noise(stream_key, extent, scale, reach, shards=(), held_as=jnp.bfloat16):
    values = jax.random.normal(stream_key, extent, jnp.float32) * scale
    if len(shards) > 0:
        values = shard_levels(stream_key, extent, shards, -0.22, 0.18) * values
    return jnp.clip(values, min=-reach, max=reach).astype(held_as)


def setup_inputs(seed: int = 0) -> dict:
    key_of = jax.random.split(jax.random.key(seed), 18)
    return {
        "hidden": noise(key_of[0], (TOKENS, D), 1.0, 6.0, ((0, 32),)),
        "segments": draw_segments(jax.random.fold_in(key_of[17], 71), 0),
        "norm_gain": jnp.clip(1.0 + 0.1 * jax.random.normal(key_of[2], (D,), jnp.float32), 0.5, 1.5),
        "proj_gate": noise(key_of[3], (D, DI), D ** -0.5, 0.21875, ((0, 16), (1, 2))),
        "proj_value": noise(key_of[4], (D, DI), D ** -0.5, 0.21875, ((0, 16), (1, 2))),
        "proj_bc": noise(key_of[5], (D, 2 * N), D ** -0.5, 0.21875, ((0, 32),)),
        "proj_step": noise(key_of[6], (D, H), D ** -0.5, 0.21875, ((0, 16), (1, 2))),
        "conv_value": noise(key_of[7], (K, DI), K ** -0.5, 3.0, ((1, 2),), jnp.float32),
        "conv_bc": noise(key_of[8], (K, 2 * N), K ** -0.5, 3.0, (), jnp.float32),
        "conv_value_bias": noise(key_of[9], (DI,), 0.5, 3.0, ((0, 2),), jnp.float32),
        "conv_bc_bias": noise(key_of[10], (2 * N,), 0.5, 3.0, (), jnp.float32),
        "step_bias": jnp.clip(-5.0 + 4.0 * jax.random.uniform(key_of[11], (H,), jnp.float32) ** shard_levels(key_of[11], (H,), ((0, 2),), -0.2, 0.2), -5.0, -1.0),
        "decay_log": jnp.clip(-3.0 + 4.0 * jax.random.uniform(key_of[12], (H,), jnp.float32) ** shard_levels(key_of[12], (H,), ((0, 2),), -0.2, 0.2), -3.0, 1.0),
        "skip_gain": jnp.clip(2.0 * jax.random.uniform(key_of[13], (H,), jnp.float32) ** shard_levels(key_of[13], (H,), ((0, 2),), -0.2, 0.2), 0.0, 2.0),
        "gate_gain": jnp.clip(1.0 + 0.1 * jax.random.normal(key_of[14], (DI,), jnp.float32), 0.5, 1.5),
        "out_weight": noise(key_of[15], (D, DI), DI ** -0.5, 0.15625, ((0, 16), (1, 2))),
        "cotangent": noise(key_of[16], (TOKENS, D), 1.0, 6.0, ((0, 32),)),
    }


@jax.custom_vjp
def low(v):
    return lax.optimization_barrier(v.astype(jnp.bfloat16)).astype(jnp.float32)

@jax.custom_vjp
def low_back(v):
    return v

def low_keep(v):
    return (low(v), None)

def low_pass(kept, grad):
    return (grad,)

def back_keep(v):
    return (v, None)

def back_low(kept, grad):
    return (low(grad),)
low.defvjp(low_keep, low_pass)
low_back.defvjp(back_keep, back_low)
EPS = 1e-05
HIGH = lax.Precision.HIGHEST

def conv_mix(stream, weight, offset, seg_row):
    width = weight.shape[0]
    length = stream.shape[0]
    padded = jnp.concatenate([jnp.zeros((width - 1, stream.shape[1]), stream.dtype), stream], 0)
    seg_pad = jnp.concatenate([jnp.full((width - 1,), -1, jnp.int32), seg_row.astype(jnp.int32)], 0)
    summed = offset[None, :] + jnp.zeros_like(stream)
    for shift_by in range(width):
        first_row = width - 1 - shift_by
        window = padded[first_row:first_row + length]
        same_doc = (seg_pad[first_row:first_row + length] == seg_row).astype(stream.dtype)
        summed = summed + weight[width - 1 - shift_by][None, :] * window * same_doc[:, None]
    return summed

def block_scan(values, b_rows, c_rows, step_rows, seg_row, decay_rate):
    length, head_count, head_size = values.shape
    state_width = b_rows.shape[1]
    blocks = length // GROUP
    seg_blocks = seg_row.reshape(blocks, GROUP).astype(jnp.int32)
    prev_segs = jnp.concatenate([jnp.full((1,), -1, jnp.int32), seg_blocks[:-1, GROUP - 1]], 0)
    causal = jnp.arange(GROUP)[:, None] >= jnp.arange(GROUP)[None, :]

    def scan_step(carried, block_item):
        x_block, b_block, c_block, dt_block, seg_block, prev_seg = block_item
        cum_rate = jnp.cumsum(dt_block * decay_rate[None, :], axis=0)
        keep_mask = causal & (seg_block[:, None] == seg_block[None, :])
        exponent = jnp.where(keep_mask[None], cum_rate.T[:, :, None] - cum_rate.T[:, None, :], -jnp.inf)
        decay_in = jnp.exp(exponent)
        scores = jnp.dot(c_block, b_block.T, precision=HIGH)
        mixing = scores[None] * decay_in
        x_scaled = x_block * dt_block[:, :, None]
        y_inner = jnp.einsum('hts,shp->thp', mixing, x_scaled, precision=HIGH)
        carry_ok = (seg_block == prev_seg).astype(values.dtype)
        y_state = jnp.einsum('tn,hnp->thp', c_block, carried, precision=HIGH)
        y_state = y_state * (jnp.exp(cum_rate) * carry_ok[:, None])[:, :, None]
        block_total = cum_rate[GROUP - 1]
        tail_decay = jnp.exp(block_total[None, :] - cum_rate) * (seg_block == seg_block[GROUP - 1]).astype(values.dtype)[:, None]
        keep_state = jnp.exp(block_total) * (seg_block[GROUP - 1] == prev_seg).astype(values.dtype)
        new_state = carried * keep_state[:, None, None] + jnp.einsum('sn,shp->hnp', b_block, x_scaled * tail_decay[:, :, None], precision=HIGH)
        return (new_state, y_inner + y_state)
    start_state = jnp.zeros((head_count, state_width, head_size), values.dtype)
    block_inputs = (values.reshape(blocks, GROUP, head_count, head_size), b_rows.reshape(blocks, GROUP, state_width), c_rows.reshape(blocks, GROUP, state_width), step_rows.reshape(blocks, GROUP, head_count), seg_blocks, prev_segs)
    _, outputs = lax.scan(jax.checkpoint(scan_step), start_state, block_inputs)
    return outputs.reshape(length, head_count, head_size)

def mixer(pre_gate, pre_value, pre_bc, pre_step, conv_value, conv_bc, conv_value_bias, conv_bc_bias, step_bias, decay_log, skip_gain, seg_row):
    length, inner_width = pre_value.shape
    head_count = pre_step.shape[1]
    head_size = inner_width // head_count
    state_width = pre_bc.shape[1] // 2
    stream = jnp.concatenate([pre_value, pre_bc], 1)
    taps = jnp.concatenate([conv_value, conv_bc], 1)
    offset = jnp.concatenate([conv_value_bias, conv_bc_bias], 0)
    activated = jax.nn.silu(conv_mix(stream, taps, offset, seg_row))
    values = activated[:, :inner_width].reshape(length, head_count, head_size)
    b_rows = activated[:, inner_width:inner_width + state_width]
    c_rows = activated[:, inner_width + state_width:]
    step_rows = jax.nn.softplus(pre_step + step_bias[None, :])
    decay_rate = -jnp.exp(decay_log)
    ssm_out = block_scan(values, b_rows, c_rows, step_rows, seg_row, decay_rate) + skip_gain[None, :, None] * values
    return ssm_out.reshape(length, inner_width) * jax.nn.silu(pre_gate)

def forward(hidden, norm_gain, proj_gate, proj_value, proj_bc, proj_step, conv_value, conv_bc, conv_value_bias, conv_bc_bias, step_bias, decay_log, skip_gain, gate_gain, out_weight, seg_part):
    seq_count, length = seg_part.shape
    normed = low(hidden * lax.rsqrt(lax.optimization_barrier(jnp.mean(hidden * hidden, -1, keepdims=True)) + EPS) * norm_gain[None, :])
    pre_gate = low_back(jnp.dot(normed, proj_gate, precision=HIGH)).reshape(seq_count, length, -1)
    pre_value = low_back(jnp.dot(normed, proj_value, precision=HIGH)).reshape(seq_count, length, -1)
    pre_bc = low_back(jnp.dot(normed, proj_bc, precision=HIGH)).reshape(seq_count, length, -1)
    pre_step = low_back(jnp.dot(normed, proj_step, precision=HIGH)).reshape(seq_count, length, -1)
    mapped = jax.vmap(mixer, in_axes=(0, 0, 0, 0, None, None, None, None, None, None, None, 0))
    gated = mapped(pre_gate, pre_value, pre_bc, pre_step, conv_value, conv_bc, conv_value_bias, conv_bc_bias, step_bias, decay_log, skip_gain, seg_part)
    gated = gated.reshape(seq_count * length, -1)
    branch_in = low(gated * lax.rsqrt(lax.optimization_barrier(jnp.mean(gated * gated, -1, keepdims=True)) + EPS) * gate_gain[None, :])
    return hidden + jnp.dot(branch_in, out_weight.T, precision=HIGH)

def reference(hidden, segments, norm_gain, proj_gate, proj_value, proj_bc, proj_step, conv_value, conv_bc, conv_value_bias, conv_bc_bias, step_bias, decay_log, skip_gain, gate_gain, out_weight, cotangent):
    params = tuple((param_item.astype(jnp.float32) for param_item in (norm_gain, proj_gate, proj_value, proj_bc, proj_step, conv_value, conv_bc, conv_value_bias, conv_bc_bias, step_bias, decay_log, skip_gain, gate_gain, out_weight)))
    seq_total = segments.shape[0]
    block_seqs = math.gcd(4, seq_total)
    block_total = seq_total // block_seqs
    hidden_blocks = hidden.astype(jnp.float32).reshape(block_total, block_seqs * LEN, D)
    cot_blocks = cotangent.astype(jnp.float32).reshape(block_total, block_seqs * LEN, D)
    seg_blocks = segments.astype(jnp.int32).reshape(block_total, block_seqs, LEN)

    def one_block(summed, block_item):
        hidden_part, cot_part, seg_part = block_item

        def run_block(hidden_in, *weights_in):
            return forward(hidden_in, *weights_in, seg_part)
        out_part, pull_back = jax.vjp(run_block, hidden_part, *params)
        grads_all = pull_back(cot_part)
        summed = tuple((left + right for left, right in zip(summed, grads_all[1:])))
        return (summed, (out_part, grads_all[0]))
    start_sums = tuple((jnp.zeros_like(param_item) for param_item in params))
    summed, (out_blocks, grad_blocks) = lax.scan(one_block, start_sums, (hidden_blocks, cot_blocks, seg_blocks))
    return (out_blocks.reshape(-1, D).astype(jnp.bfloat16), grad_blocks.reshape(-1, D), summed[0], summed[1], summed[2], summed[3], summed[4], summed[5], summed[6], summed[7], summed[8], summed[9], summed[10], summed[11], summed[12], summed[13])
```

```python
import jax
import jax.numpy as jnp
from jax import lax
from jax.experimental import pallas as pl
from jax.experimental.pallas import tpu as pltpu
from jax.sharding import PartitionSpec as P

D = 768
GROUP = 256
DI = 1536


EPS = 1e-05
HIGH = lax.Precision.HIGHEST


def conv_mix(stream, weight, offset, seg_row):
    width = weight.shape[0]
    length = stream.shape[0]
    padded = jnp.concatenate([jnp.zeros((width - 1, stream.shape[1]), stream.dtype), stream], 0)
    seg_pad = jnp.concatenate([jnp.full((width - 1,), -1, jnp.int32), seg_row], 0)
    summed = offset[None, :] + jnp.zeros_like(stream)
    for shift_by in range(width):
        first_row = width - 1 - shift_by
        window = padded[first_row : first_row + length]
        same_doc = (seg_pad[first_row : first_row + length] == seg_row).astype(stream.dtype)
        summed = summed + weight[width - 1 - shift_by][None, :] * window * same_doc[:, None]
    return summed


def block_scan_state(values, b_rows, c_rows, step_rows, seg_row, decay_rate):
    length, head_count, head_size = values.shape
    state_width = b_rows.shape[1]
    blocks = length // GROUP
    seg_blocks = seg_row.reshape(blocks, GROUP)
    prev_segs = jnp.concatenate([jnp.full((1,), -1, jnp.int32), seg_blocks[:-1, GROUP - 1]], 0)
    causal = jnp.arange(GROUP)[:, None] >= jnp.arange(GROUP)[None, :]

    def scan_step(carried, block_item):
        x_block, b_block, c_block, dt_block, seg_block, prev_seg = block_item
        cum_rate = jnp.cumsum(dt_block * decay_rate[None, :], axis=0)
        keep_mask = causal & (seg_block[:, None] == seg_block[None, :])
        exponent = jnp.where(
            keep_mask[None], cum_rate.T[:, :, None] - cum_rate.T[:, None, :], -jnp.inf
        )
        decay_in = jnp.exp(exponent)
        scores = jnp.dot(c_block, b_block.T, precision=HIGH)
        mixing = scores[None] * decay_in
        x_scaled = x_block * dt_block[:, :, None]
        y_inner = jnp.einsum("hts,shp->thp", mixing, x_scaled, precision=HIGH)
        carry_ok = (seg_block == prev_seg).astype(values.dtype)
        y_state = jnp.einsum("tn,hnp->thp", c_block, carried, precision=HIGH)
        y_state = y_state * (jnp.exp(cum_rate) * carry_ok[:, None])[:, :, None]
        block_total = cum_rate[GROUP - 1]
        tail_decay = (
            jnp.exp(block_total[None, :] - cum_rate)
            * (seg_block == seg_block[GROUP - 1]).astype(values.dtype)[:, None]
        )
        keep_state = jnp.exp(block_total) * (seg_block[GROUP - 1] == prev_seg).astype(values.dtype)
        new_state = carried * keep_state[:, None, None] + jnp.einsum(
            "sn,shp->hnp", b_block, x_scaled * tail_decay[:, :, None], precision=HIGH
        )
        return (new_state, y_inner + y_state)

    start_state = jnp.zeros((head_count, state_width, head_size), values.dtype)
    block_inputs = (
        values.reshape(blocks, GROUP, head_count, head_size),
        b_rows.reshape(blocks, GROUP, state_width),
        c_rows.reshape(blocks, GROUP, state_width),
        step_rows.reshape(blocks, GROUP, head_count),
        seg_blocks,
        prev_segs,
    )
    final_state, outputs = lax.scan(jax.checkpoint(scan_step), start_state, block_inputs)
    return (outputs.reshape(length, head_count, head_size), final_state)


def mixer(
    pre_gate,
    pre_value,
    pre_bc,
    pre_step,
    conv_value,
    conv_bc,
    conv_value_bias,
    conv_bc_bias,
    step_bias,
    decay_log,
    skip_gain,
    seg_row,
):
    length, inner_width = pre_value.shape
    head_count = pre_step.shape[1]
    head_size = inner_width // head_count
    state_width = pre_bc.shape[1] // 2
    stream = jnp.concatenate([pre_value, pre_bc], 1)
    taps = jnp.concatenate([conv_value, conv_bc], 1)
    offset = jnp.concatenate([conv_value_bias, conv_bc_bias], 0)
    activated = jax.nn.silu(conv_mix(stream, taps, offset, seg_row))
    values = activated[:, :inner_width].reshape(length, head_count, head_size)
    b_rows = activated[:, inner_width : inner_width + state_width]
    c_rows = activated[:, inner_width + state_width :]
    step_rows = jax.nn.softplus(pre_step + step_bias[None, :])
    decay_rate = -jnp.exp(decay_log)
    scanned, _ = block_scan_state(values, b_rows, c_rows, step_rows, seg_row, decay_rate)
    ssm_out = scanned + skip_gain[None, :, None] * values
    return ssm_out.reshape(length, inner_width) * jax.nn.silu(pre_gate)


def contract_rows(left, right):
    return lax.dot_general(
        left, right, (((0,), (0,)), ((), ())), preferred_element_type=jnp.float32
    )


def contract_cols(left, right):
    return lax.dot_general(
        left, right, (((1,), (1,)), ((), ())), preferred_element_type=jnp.float32
    )


VMEM_LIMIT = 56 * 2**20


def flipped(index, pattern, bits):
    result = index
    for bit in bits:
        if pattern & bit:
            result = result + bit * (1 - 2 * lax.rem(index // bit, 2))
    return result


def greet(partners):
    barrier = pltpu.get_barrier_semaphore()
    for partner in partners:
        pl.semaphore_signal(
            barrier, inc=1, device_id=partner, device_id_type=pl.DeviceIdType.MESH
        )
    pl.semaphore_wait(barrier, len(partners))


def gather_kernel(bits, own_ref, full_ref, held, send_sem, recv_sem, out_sem):
    me = lax.axis_index("dp")
    greet([{"dp": flipped(me, bit, bits)} for bit in bits])
    held[me] = own_ref[...]
    copies = {}

    def forward(pattern, below):
        chunk = flipped(me, pattern, bits)
        for bit in reversed(bits):
            if bit < below:
                arrives = pattern ^ bit
                copies[arrives] = pltpu.make_async_remote_copy(
                    src_ref=held.at[chunk],
                    dst_ref=held.at[chunk],
                    send_sem=send_sem.at[arrives],
                    recv_sem=recv_sem.at[arrives],
                    device_id={"dp": flipped(me, bit, bits)},
                    device_id_type=pl.DeviceIdType.MESH,
                )
                copies[arrives].start()

    total = 2 * bits[-1]
    forward(0, total)
    for low in reversed(bits):
        for pattern in range(low, total, 2 * low):
            copies[pattern].wait_recv()
            forward(pattern, low)
    for copy in copies.values():
        copy.wait_send()
    out = pltpu.make_async_copy(held, full_ref, out_sem)
    out.start()
    out.wait()


def gather_rows(own, count):
    bits = [1 << power for power in range(count.bit_length() - 1)]
    rows, columns = own.shape
    full = pl.pallas_call(
        lambda *refs: gather_kernel(bits, *refs),
        out_shape=jax.ShapeDtypeStruct((count, rows, columns), own.dtype),
        in_specs=[pl.BlockSpec(memory_space=pltpu.VMEM)],
        out_specs=pl.BlockSpec(memory_space=pl.ANY),
        scratch_shapes=[
            pltpu.VMEM((count, rows, columns), own.dtype),
            pltpu.SemaphoreType.DMA((count,)),
            pltpu.SemaphoreType.DMA((count,)),
            pltpu.SemaphoreType.DMA,
        ],
        compiler_params=pltpu.CompilerParams(
            collective_id=0, has_side_effects=True, vmem_limit_bytes=VMEM_LIMIT
        ),
        name="gather_rows",
    )(own)
    return full.reshape(count * rows, columns)


def scatter_kernel(
    bits,
    bc_from,
    parts_ref,
    small_ref,
    sum_ref,
    bc_ref,
    small_out,
    slots,
    staged,
    bc_sum,
    bc_got,
    small_sent,
    small_got,
    send_sem,
    recv_sem,
    bc_sem,
    small_send,
    small_recv,
):
    me = lax.axis_index("dp")
    half = lax.axis_index("tensor")
    other = 1 - half
    partners = [{"dp": flipped(me, bit, bits)} for bit in bits] + [{"tensor": other}]
    greet(partners)
    total = 2 * bits[-1]
    copies = {}

    def lowest(pattern):
        return pattern & -pattern

    def send(pattern, source):
        copies[pattern] = pltpu.make_async_remote_copy(
            src_ref=source,
            dst_ref=slots.at[pattern],
            send_sem=send_sem.at[pattern],
            recv_sem=recv_sem.at[pattern],
            device_id={"dp": flipped(me, lowest(pattern), bits)},
            device_id_type=pl.DeviceIdType.MESH,
        )
        copies[pattern].start()

    def summed(pattern):
        value = parts_ref[flipped(me, pattern, bits)].astype(jnp.float32)
        for bit in bits:
            if pattern == 0 or bit < lowest(pattern):
                copies[pattern + bit].wait_recv()
                value = value + slots[pattern + bit].astype(jnp.float32)
        return value

    odd = sorted(range(1, total, 2), key=lambda p: (lowest(p - 1) if p > 1 else total, p))
    for pattern in odd:
        send(pattern, parts_ref.at[flipped(me, pattern, bits)])

    small_sent[0] = small_ref[...]
    small_copies = []

    def small_step(step):
        copy = pltpu.make_async_remote_copy(
            src_ref=small_sent.at[step],
            dst_ref=small_got.at[step],
            send_sem=small_send.at[step],
            recv_sem=small_recv.at[step],
            device_id=partners[step],
            device_id_type=pl.DeviceIdType.MESH,
        )
        copy.start()
        small_copies.append(copy)

    small_step(0)
    for step, bit in enumerate(bits[1:]):
        for pattern in range(bit, total, 2 * bit):
            staged[pattern] = summed(pattern).astype(staged.dtype)
            send(pattern, staged.at[pattern])
        small_copies[step].wait_recv()
        small_sent[step + 1] = small_sent[step] + small_got[step]
        small_step(step + 1)
    value = summed(0)
    sum_ref[...] = value
    last = len(bits)
    bc_sum[...] = value[:, bc_from : bc_from + bc_sum.shape[1]]
    span = bc_ref.shape[0]
    bc_copy = pltpu.make_async_remote_copy(
        src_ref=bc_sum.at[pl.ds(pl.multiple_of(other * span, 8), span)],
        dst_ref=bc_got,
        send_sem=bc_sem.at[0],
        recv_sem=bc_sem.at[1],
        device_id={"tensor": other},
        device_id_type=pl.DeviceIdType.MESH,
    )
    bc_copy.start()
    small_copies[last - 1].wait_recv()
    small_sent[last] = small_sent[last - 1] + small_got[last - 1]
    small_step(last)
    small_copies[last].wait_recv()
    small_out[:8] = small_sent[last, :8]
    small_out[8:] = small_sent[last, 8:] + small_got[last, 8:]
    bc_copy.wait_recv()
    bc_ref[...] = bc_sum[pl.ds(pl.multiple_of(half * span, 8), span)] + bc_got[...]
    bc_copy.wait_send()
    for copy in list(copies.values()) + small_copies:
        copy.wait_send()


def scatter_rows(parts, small, count, bc_from, bc_width):
    bits = [1 << power for power in range(count.bit_length() - 1)]
    rows, columns = parts.shape[0] // count, parts.shape[1]
    steps = len(bits) + 1
    vmem = pl.BlockSpec(memory_space=pltpu.VMEM)
    return pl.pallas_call(
        lambda *refs: scatter_kernel(bits, bc_from, *refs),
        out_shape=(
            jax.ShapeDtypeStruct((rows, columns), jnp.float32),
            jax.ShapeDtypeStruct((rows // 2, bc_width), jnp.float32),
            jax.ShapeDtypeStruct(small.shape, jnp.float32),
        ),
        in_specs=[vmem, vmem],
        out_specs=(vmem, vmem, vmem),
        scratch_shapes=[
            pltpu.VMEM((count, rows, columns), parts.dtype),
            pltpu.VMEM((count, rows, columns), parts.dtype),
            pltpu.VMEM((rows, bc_width), jnp.float32),
            pltpu.VMEM((rows // 2, bc_width), jnp.float32),
            pltpu.VMEM((steps,) + small.shape, jnp.float32),
            pltpu.VMEM((steps,) + small.shape, jnp.float32),
            pltpu.SemaphoreType.DMA((count,)),
            pltpu.SemaphoreType.DMA((count,)),
            pltpu.SemaphoreType.DMA((2,)),
            pltpu.SemaphoreType.DMA((steps,)),
            pltpu.SemaphoreType.DMA((steps,)),
        ],
        compiler_params=pltpu.CompilerParams(
            collective_id=1, has_side_effects=True, vmem_limit_bytes=VMEM_LIMIT
        ),
        name="scatter_rows",
    )(parts.reshape(count, rows, columns), small)


def swap(values):
    return lax.ppermute(values, "tensor", [(0, 1), (1, 0)])


def both_halves(own, index):
    got = swap(own)
    return jnp.where(
        index == 0, jnp.concatenate([own, got], 0), jnp.concatenate([got, own], 0)
    )


def own_half(values, index):
    span = values.shape[0] // 2
    away = lax.dynamic_slice_in_dim(values, (1 - index) * span, span, 0)
    kept = lax.dynamic_slice_in_dim(values, index * span, span, 0)
    return kept + swap(away.astype(jnp.bfloat16)).astype(jnp.float32)


def local(
    hidden,
    segments,
    norm_gain,
    proj_gate,
    proj_value,
    proj_bc,
    proj_step,
    conv_value,
    conv_bc,
    conv_value_bias,
    conv_bc_bias,
    step_bias,
    decay_log,
    skip_gain,
    gate_gain,
    out_weight,
    cotangent,
):
    seq_count, length = segments.shape
    own_index = lax.axis_index("tensor")
    count = lax.axis_size("dp")
    rows = proj_gate.shape[0]
    inner = proj_gate.shape[1]
    bc_width = proj_bc.shape[1]
    head_count = proj_step.shape[1]
    step_pad = -head_count % 128
    bc_from = 3 * inner
    step_from = bc_from + bc_width
    direct = rows % 16 == 0 and count & (count - 1) == 0
    residual = hidden.astype(jnp.float32)
    inv_rms = lax.rsqrt(jnp.mean(residual * residual, -1, keepdims=True) + EPS)
    normed = (residual * inv_rms * norm_gain[None, :]).astype(jnp.bfloat16)
    bc_pair = both_halves(proj_bc, own_index)
    own_weights = jnp.concatenate(
        [proj_value, proj_gate, out_weight, bc_pair, jnp.pad(proj_step, ((0, 0), (0, step_pad)))], 1
    )
    rows_all = both_halves(normed, own_index)
    cot_all = both_halves(cotangent, own_index)
    if direct:
        weights = gather_rows(own_weights, count)
    else:
        weights = lax.all_gather(own_weights, "dp", axis=0, tiled=True)
    value_full = weights[:, :inner]
    gate_full = weights[:, inner : 2 * inner]
    outw_full = weights[:, 2 * inner : 3 * inner]
    bc_full = weights[:, bc_from:step_from]
    step_full = weights[:, step_from:]
    pre_gate = jnp.dot(rows_all, gate_full, preferred_element_type=jnp.float32)
    pre_value = jnp.dot(rows_all, value_full, preferred_element_type=jnp.float32)
    pre_bc = jnp.dot(rows_all, bc_full, preferred_element_type=jnp.float32)
    pre_step = jnp.dot(rows_all, step_full, preferred_element_type=jnp.float32)[:, :head_count]
    grad_branch = jnp.dot(cot_all, outw_full, preferred_element_type=jnp.float32)
    weighted = grad_branch * gate_gain[None, :]

    def local_mixer(*inputs):
        return mixer(*inputs, segments.reshape(-1))

    gated, pull_back = jax.vjp(
        local_mixer,
        pre_gate,
        pre_value,
        pre_bc,
        pre_step,
        conv_value,
        conv_bc,
        conv_value_bias,
        conv_bc_bias,
        step_bias,
        decay_log,
        skip_gain,
    )
    sums = jnp.stack([jnp.sum(gated * gated, -1), jnp.sum(weighted * gated, -1)], 0)
    sums = sums + swap(sums)
    inv_gate = lax.rsqrt(sums[0] / DI + EPS)[:, None]
    cross = (sums[1] / DI)[:, None]
    branch_in = (gated * inv_gate * gate_gain[None, :]).astype(jnp.bfloat16)
    branch = own_half(contract_cols(branch_in, outw_full), own_index)
    mixed_out = (residual + branch).astype(jnp.bfloat16)
    grad_out_w = contract_rows(cot_all, branch_in)
    grad_gate_gain = jnp.sum(grad_branch * gated * inv_gate, 0)
    grad_gated = inv_gate * weighted - gated * inv_gate**3 * cross
    (
        grad_pg,
        grad_pv,
        grad_pbc,
        grad_ps,
        grad_cv,
        grad_cbc,
        grad_cvb,
        grad_cbcb,
        grad_sb,
        grad_dl,
        grad_sk,
    ) = pull_back(grad_gated)
    low_gate = grad_pg.astype(jnp.bfloat16)
    low_value = grad_pv.astype(jnp.bfloat16)
    low_step = jnp.pad(grad_ps, ((0, 0), (0, step_pad))).astype(jnp.bfloat16)
    grad_rows = contract_cols(low_gate, gate_full) + contract_cols(low_value, value_full)
    grad_rows = grad_rows + contract_cols(low_step, step_full)
    grad_rows_own = own_half(grad_rows, own_index)
    low_bc = own_half(grad_pbc, own_index).astype(jnp.bfloat16)
    grad_normed = grad_rows_own + contract_cols(low_bc, bc_full)
    weighted_in = grad_normed * norm_gain[None, :]
    grad_norm_part = jnp.sum(grad_normed * residual * inv_rms, 0)
    grad_input = (
        cotangent.astype(jnp.float32)
        + inv_rms * weighted_in
        - residual * inv_rms**3 * jnp.sum(weighted_in * residual, -1, keepdims=True) / D
    )
    parts = jnp.concatenate(
        [
            contract_rows(rows_all, low_value),
            contract_rows(rows_all, low_gate),
            grad_out_w,
            contract_rows(normed, low_bc),
            contract_rows(rows_all, low_step),
        ],
        1,
    )

    def as_row(values):
        flat = values.reshape(1, -1)
        return jnp.pad(flat, ((0, 0), (0, inner - flat.shape[1])))

    bc_rows = -(-4 * bc_width // inner)
    small = jnp.concatenate(
        [
            grad_cv,
            as_row(grad_cvb),
            as_row(grad_gate_gain),
            as_row(jnp.concatenate([grad_sb, grad_dl, grad_sk])),
            as_row(grad_norm_part[:0]),
            as_row(grad_norm_part),
            as_row(grad_cbcb),
            jnp.pad(grad_cbc.reshape(-1), (0, bc_rows * inner - 4 * bc_width)).reshape(bc_rows, inner),
            jnp.zeros((6 - bc_rows, inner), jnp.float32),
        ],
        0,
    )
    if direct:
        gw, gw_bc, small = scatter_rows(parts.astype(jnp.bfloat16), small, count, bc_from, bc_width)
    else:
        gw = lax.psum_scatter(parts, "dp", scatter_dimension=0, tiled=True)
        gw_bc = lax.psum_scatter(
            gw[:, bc_from:step_from], "tensor", scatter_dimension=0, tiled=True
        )
        small = lax.psum(small, "dp")
        small = jnp.concatenate([small[:8], lax.psum(small[8:], "tensor")], 0)
    heads = small[6]
    return (
        mixed_out,
        grad_input,
        small[8],
        gw[:, inner : 2 * inner],
        gw[:, :inner],
        gw_bc,
        gw[:, step_from : step_from + head_count],
        small[:4],
        small[10 : 10 + bc_rows].reshape(-1)[: 4 * bc_width].reshape(4, bc_width),
        small[4],
        small[9, :bc_width],
        heads[:head_count],
        heads[head_count : 2 * head_count],
        heads[2 * head_count : 3 * head_count],
        small[5],
        gw[:, 2 * inner : 3 * inner],
    )


def solution(mesh):
    in_specs = (
        P(("dp", "tensor"), None),
        P("dp", None),
        P(),
        P("dp", "tensor"),
        P("dp", "tensor"),
        P(("dp", "tensor"), None),
        P("dp", "tensor"),
        P(None, "tensor"),
        P(),
        P("tensor"),
        P(),
        P("tensor"),
        P("tensor"),
        P("tensor"),
        P("tensor"),
        P("dp", "tensor"),
        P(("dp", "tensor"), None),
    )
    out_specs = (
        P(("dp", "tensor"), None),
        P(("dp", "tensor"), None),
        P(),
        P("dp", "tensor"),
        P("dp", "tensor"),
        P(("dp", "tensor"), None),
        P("dp", "tensor"),
        P(None, "tensor"),
        P(),
        P("tensor"),
        P(),
        P("tensor"),
        P("tensor"),
        P("tensor"),
        P("tensor"),
        P("dp", "tensor"),
    )
    return jax.shard_map(local, mesh=mesh, in_specs=in_specs, out_specs=out_specs, check_vma=False)
```

```python
import jax
import jax.numpy as jnp
from jax import lax
from jax.experimental import pallas as pl
from jax.experimental.pallas import tpu as pltpu
from jax.sharding import PartitionSpec as P

D = 768
GROUP = 256
DI = 1536


EPS = 1e-05
HIGH = lax.Precision.HIGHEST


def conv_mix(stream, weight, offset, seg_row):
    width = weight.shape[0]
    length = stream.shape[0]
    padded = jnp.concatenate([jnp.zeros((width - 1, stream.shape[1]), stream.dtype), stream], 0)
    seg_pad = jnp.concatenate([jnp.full((width - 1,), -1, jnp.int32), seg_row], 0)
    summed = offset[None, :] + jnp.zeros_like(stream)
    for shift_by in range(width):
        first_row = width - 1 - shift_by
        window = padded[first_row : first_row + length]
        same_doc = (seg_pad[first_row : first_row + length] == seg_row).astype(stream.dtype)
        summed = summed + weight[width - 1 - shift_by][None, :] * window * same_doc[:, None]
    return summed


def contract_rows(left, right):
    return lax.dot_general(
        left, right, (((0,), (0,)), ((), ())), preferred_element_type=jnp.float32
    )


def contract_cols(left, right):
    return lax.dot_general(
        left, right, (((1,), (1,)), ((), ())), preferred_element_type=jnp.float32
    )


VMEM_LIMIT = 56 * 2**20


def flipped(index, pattern, bits):
    result = index
    for bit in bits:
        if pattern & bit:
            result = result + bit * (1 - 2 * lax.rem(index // bit, 2))
    return result


def greet(partners):
    barrier = pltpu.get_barrier_semaphore()
    for partner in partners:
        pl.semaphore_signal(
            barrier, inc=1, device_id=partner, device_id_type=pl.DeviceIdType.MESH
        )
    pl.semaphore_wait(barrier, len(partners))


def gather_kernel(bits, own_ref, full_ref, held, send_sem, recv_sem, out_sem):
    me = lax.axis_index("dp")
    greet([{"dp": flipped(me, bit, bits)} for bit in bits])
    held[me] = own_ref[...]
    copies = {}

    def forward(pattern, below):
        chunk = flipped(me, pattern, bits)
        for bit in reversed(bits):
            if bit < below:
                arrives = pattern ^ bit
                copies[arrives] = pltpu.make_async_remote_copy(
                    src_ref=held.at[chunk],
                    dst_ref=held.at[chunk],
                    send_sem=send_sem.at[arrives],
                    recv_sem=recv_sem.at[arrives],
                    device_id={"dp": flipped(me, bit, bits)},
                    device_id_type=pl.DeviceIdType.MESH,
                )
                copies[arrives].start()

    total = 2 * bits[-1]
    forward(0, total)
    for low in reversed(bits):
        for pattern in range(low, total, 2 * low):
            copies[pattern].wait_recv()
            forward(pattern, low)
    for copy in copies.values():
        copy.wait_send()
    out = pltpu.make_async_copy(held, full_ref, out_sem)
    out.start()
    out.wait()


def gather_rows(own, count):
    bits = [1 << power for power in range(count.bit_length() - 1)]
    rows, columns = own.shape
    full = pl.pallas_call(
        lambda *refs: gather_kernel(bits, *refs),
        out_shape=jax.ShapeDtypeStruct((count, rows, columns), own.dtype),
        in_specs=[pl.BlockSpec(memory_space=pltpu.VMEM)],
        out_specs=pl.BlockSpec(memory_space=pl.ANY),
        scratch_shapes=[
            pltpu.VMEM((count, rows, columns), own.dtype),
            pltpu.SemaphoreType.DMA((count,)),
            pltpu.SemaphoreType.DMA((count,)),
            pltpu.SemaphoreType.DMA,
        ],
        compiler_params=pltpu.CompilerParams(
            collective_id=0, has_side_effects=True, vmem_limit_bytes=VMEM_LIMIT
        ),
        name="gather_rows",
    )(own)
    return full.reshape(count * rows, columns)


def scatter_kernel(
    bits,
    bc_from,
    parts_ref,
    small_ref,
    sum_ref,
    bc_ref,
    small_out,
    slots,
    staged,
    bc_sum,
    bc_got,
    small_sent,
    small_got,
    send_sem,
    recv_sem,
    bc_sem,
    small_send,
    small_recv,
):
    me = lax.axis_index("dp")
    half = lax.axis_index("tensor")
    other = 1 - half
    partners = [{"dp": flipped(me, bit, bits)} for bit in bits] + [{"tensor": other}]
    greet(partners)
    total = 2 * bits[-1]
    copies = {}

    def lowest(pattern):
        return pattern & -pattern

    def send(pattern, source):
        copies[pattern] = pltpu.make_async_remote_copy(
            src_ref=source,
            dst_ref=slots.at[pattern],
            send_sem=send_sem.at[pattern],
            recv_sem=recv_sem.at[pattern],
            device_id={"dp": flipped(me, lowest(pattern), bits)},
            device_id_type=pl.DeviceIdType.MESH,
        )
        copies[pattern].start()

    def summed(pattern):
        value = parts_ref[flipped(me, pattern, bits)].astype(jnp.float32)
        for bit in bits:
            if pattern == 0 or bit < lowest(pattern):
                copies[pattern + bit].wait_recv()
                value = value + slots[pattern + bit].astype(jnp.float32)
        return value

    odd = sorted(range(1, total, 2), key=lambda p: (lowest(p - 1) if p > 1 else total, p))
    for pattern in odd:
        send(pattern, parts_ref.at[flipped(me, pattern, bits)])

    small_sent[0] = small_ref[...]
    small_copies = []

    def small_step(step):
        copy = pltpu.make_async_remote_copy(
            src_ref=small_sent.at[step],
            dst_ref=small_got.at[step],
            send_sem=small_send.at[step],
            recv_sem=small_recv.at[step],
            device_id=partners[step],
            device_id_type=pl.DeviceIdType.MESH,
        )
        copy.start()
        small_copies.append(copy)

    small_step(0)
    for step, bit in enumerate(bits[1:]):
        for pattern in range(bit, total, 2 * bit):
            staged[pattern] = summed(pattern).astype(staged.dtype)
            send(pattern, staged.at[pattern])
        small_copies[step].wait_recv()
        small_sent[step + 1] = small_sent[step] + small_got[step]
        small_step(step + 1)
    value = summed(0)
    sum_ref[...] = value
    last = len(bits)
    bc_sum[...] = value[:, bc_from : bc_from + bc_sum.shape[1]]
    span = bc_ref.shape[0]
    bc_copy = pltpu.make_async_remote_copy(
        src_ref=bc_sum.at[pl.ds(pl.multiple_of(other * span, 8), span)],
        dst_ref=bc_got,
        send_sem=bc_sem.at[0],
        recv_sem=bc_sem.at[1],
        device_id={"tensor": other},
        device_id_type=pl.DeviceIdType.MESH,
    )
    bc_copy.start()
    small_copies[last - 1].wait_recv()
    small_sent[last] = small_sent[last - 1] + small_got[last - 1]
    small_step(last)
    small_copies[last].wait_recv()
    small_out[:8] = small_sent[last, :8]
    small_out[8:] = small_sent[last, 8:] + small_got[last, 8:]
    bc_copy.wait_recv()
    bc_ref[...] = bc_sum[pl.ds(pl.multiple_of(half * span, 8), span)] + bc_got[...]
    bc_copy.wait_send()
    for copy in list(copies.values()) + small_copies:
        copy.wait_send()


def scatter_rows(parts, small, count, bc_from, bc_width):
    bits = [1 << power for power in range(count.bit_length() - 1)]
    rows, columns = parts.shape[0] // count, parts.shape[1]
    steps = len(bits) + 1
    vmem = pl.BlockSpec(memory_space=pltpu.VMEM)
    return pl.pallas_call(
        lambda *refs: scatter_kernel(bits, bc_from, *refs),
        out_shape=(
            jax.ShapeDtypeStruct((rows, columns), jnp.float32),
            jax.ShapeDtypeStruct((rows // 2, bc_width), jnp.float32),
            jax.ShapeDtypeStruct(small.shape, jnp.float32),
        ),
        in_specs=[vmem, vmem],
        out_specs=(vmem, vmem, vmem),
        scratch_shapes=[
            pltpu.VMEM((count, rows, columns), parts.dtype),
            pltpu.VMEM((count, rows, columns), parts.dtype),
            pltpu.VMEM((rows, bc_width), jnp.float32),
            pltpu.VMEM((rows // 2, bc_width), jnp.float32),
            pltpu.VMEM((steps,) + small.shape, jnp.float32),
            pltpu.VMEM((steps,) + small.shape, jnp.float32),
            pltpu.SemaphoreType.DMA((count,)),
            pltpu.SemaphoreType.DMA((count,)),
            pltpu.SemaphoreType.DMA((2,)),
            pltpu.SemaphoreType.DMA((steps,)),
            pltpu.SemaphoreType.DMA((steps,)),
        ],
        compiler_params=pltpu.CompilerParams(
            collective_id=1, has_side_effects=True, vmem_limit_bytes=VMEM_LIMIT
        ),
        name="scatter_rows",
    )(parts.reshape(count, rows, columns), small)


def swap(values):
    return lax.ppermute(values, "tensor", [(0, 1), (1, 0)])


def both_halves(own, index):
    got = swap(own)
    return jnp.where(
        index == 0, jnp.concatenate([own, got], 0), jnp.concatenate([got, own], 0)
    )


def own_half(values, index):
    span = values.shape[0] // 2
    away = lax.dynamic_slice_in_dim(values, (1 - index) * span, span, 0)
    kept = lax.dynamic_slice_in_dim(values, index * span, span, 0)
    return kept + swap(away.astype(jnp.bfloat16)).astype(jnp.float32)


def mm(left, right, left_dim, right_dim, both=True):
    def one(first, second):
        return lax.dot_general(
            first,
            second,
            (((left_dim,), (right_dim,)), ((), ())),
            preferred_element_type=jnp.float32,
        )

    def split(values):
        high = values.astype(jnp.bfloat16)
        return high, (values - high.astype(jnp.float32)).astype(jnp.bfloat16)

    left_high, left_low = split(left)
    right_high, right_low = split(right)
    if not both:
        return one(left_high, right_high)
    return one(left_high, right_high) + (one(left_high, right_low) + one(left_low, right_high))


def shifted(values, by):
    if by == 0:
        return values
    return pltpu.roll(values, by % values.shape[0], 0)


def conv_pair(stream, masks, taps_ref, offset_ref):
    width = taps_ref.shape[0]
    summed = offset_ref[...] + taps_ref[width - 1 : width, :] * stream
    for by in range(1, width):
        window = shifted(stream, by) * masks[:, by - 1 : by]
        summed = summed + taps_ref[width - 1 - by : width - by, :] * window
    return summed


def pair_cols(first, second, span, head_size):
    lane = lax.broadcasted_iota(jnp.int32, (span, 2 * head_size), 1)
    return jnp.where(lane < head_size, first, second)


def keep_pairs(seg_col, seg_row):
    span = seg_col.shape[0]
    later = lax.broadcasted_iota(jnp.int32, (span, span), 0)
    earlier = lax.broadcasted_iota(jnp.int32, (span, span), 1)
    return (later >= earlier) & (seg_col == seg_row)


def block_terms(block, cols_ref, masks_ref, head_size):
    rows = pl.ds(block * GROUP, GROUP)
    cum0, cum1 = cols_ref[0, rows, 0:1], cols_ref[0, rows, 1:2]
    last = pl.ds(block * GROUP + GROUP - 1, 1)
    tot0, tot1 = cols_ref[0, last, 0:1], cols_ref[0, last, 1:2]
    step = pair_cols(cols_ref[0, rows, 2:3], cols_ref[0, rows, 3:4], GROUP, head_size)
    tail = jnp.exp(pair_cols(tot0 - cum0, tot1 - cum1, GROUP, head_size)) * masks_ref[rows, 4:5]
    enter = jnp.exp(pair_cols(cum0, cum1, GROUP, head_size)) * masks_ref[rows, 3:4]
    keep = jnp.exp(pair_cols(tot0, tot1, 1, head_size)) * masks_ref[last, 5:6]
    return rows, cum0, cum1, step, tail, enter, keep


def forward_kernel(
    head_size,
    value_ref,
    gate_ref,
    branch_ref,
    bc_ref,
    cols_ref,
    rows_ref,
    masks_ref,
    seg_col_ref,
    seg_row_ref,
    taps_ref,
    offset_ref,
    skip_ref,
    gain_ref,
    gated_ref,
    ssm_ref,
    states_ref,
    sums_ref,
    scores,
    mixed_x,
):
    length, state_width = value_ref.shape[0], bc_ref.shape[1] // 2
    first = pl.program_id(0) == 0

    @pl.when(first)
    def _():
        sums_ref[...] = jnp.zeros_like(sums_ref)
        for block in range(length // GROUP):
            rows = pl.ds(block * GROUP, GROUP)
            raw = mm(bc_ref[rows, state_width:], bc_ref[rows, :state_width], 1, 1)
            scores[block] = jnp.where(keep_pairs(seg_col_ref[rows, :], seg_row_ref[:, rows]), raw, 0.0)

    conv = conv_pair(value_ref[...], masks_ref[...], taps_ref, offset_ref)
    mixed_x[...] = conv * jax.nn.sigmoid(conv)
    state = jnp.zeros((state_width, 2 * head_size), jnp.float32)
    for block in range(length // GROUP):
        rows, cum0, cum1, step, tail, enter, keep = block_terms(
            block, cols_ref, masks_ref, head_size
        )
        x = mixed_x[rows, :]
        x_step = x * step
        score = scores[block]
        mix0 = score * jnp.exp(jnp.minimum(cum0 - rows_ref[0, 0:1, rows], 0.0))
        mix1 = score * jnp.exp(jnp.minimum(cum1 - rows_ref[0, 1:2, rows], 0.0))
        y = pair_cols(
            mm(mix0, x_step, 1, 0),
            mm(mix1, x_step, 1, 0),
            GROUP,
            head_size,
        )
        states_ref[0, block] = state
        if block > 0:
            y = y + mm(bc_ref[rows, state_width:], state, 1, 0) * enter
        grown = mm(bc_ref[rows, :state_width], (x_step * tail), 0, 0)
        state = state * keep + grown
        ssm = y + skip_ref[...] * x
        gate = gate_ref[rows, :]
        gated = ssm * (gate * jax.nn.sigmoid(gate))
        ssm_ref[rows, :] = ssm
        gated_ref[rows, :] = gated
        sums_ref[rows, 0:1] += jnp.sum(gated * gated, 1, keepdims=True)
        weighted = branch_ref[rows, :] * gain_ref[...]
        sums_ref[rows, 1:2] += jnp.sum(gated * weighted, 1, keepdims=True)


def backward_kernel(
    head_size,
    value_ref,
    gate_ref,
    branch_ref,
    ssm_ref,
    states_ref,
    norm_ref,
    bc_ref,
    cols_ref,
    rows_ref,
    masks_ref,
    seg_col_ref,
    seg_row_ref,
    taps_ref,
    offset_ref,
    skip_ref,
    gain_ref,
    grad_gate_ref,
    grad_value_ref,
    grad_bc_ref,
    grad_cols_ref,
    params_ref,
    scores,
    grad_scores,
    mixed_x,
    slope,
    grad_y,
):
    length, state_width = value_ref.shape[0], bc_ref.shape[1] // 2
    blocks = length // GROUP
    width = taps_ref.shape[0]

    @pl.when(pl.program_id(0) == 0)
    def _():
        grad_bc_ref[...] = jnp.zeros_like(grad_bc_ref)
        grad_scores[...] = jnp.zeros_like(grad_scores)
        for block in range(blocks):
            rows = pl.ds(block * GROUP, GROUP)
            raw = mm(bc_ref[rows, state_width:], bc_ref[rows, :state_width], 1, 1)
            scores[block] = jnp.where(keep_pairs(seg_col_ref[rows, :], seg_row_ref[:, rows]), raw, 0.0)

    conv = conv_pair(value_ref[...], masks_ref[...], taps_ref, offset_ref)
    sig = jax.nn.sigmoid(conv)
    mixed_x[...] = conv * sig
    slope[...] = sig * (1.0 + conv * (1.0 - sig))
    gate = gate_ref[...]
    gate_sig = jax.nn.sigmoid(gate)
    ssm = ssm_ref[...]
    gated = ssm * (gate * gate_sig)
    inv_gate = norm_ref[:, 0:1]
    branch = branch_ref[...]
    grad_gated = inv_gate * (branch * gain_ref[...]) - gated * norm_ref[:, 1:2]
    grad_gate_ref[...] = (
        grad_gated * ssm * (gate_sig * (1.0 + gate * (1.0 - gate_sig)))
    ).astype(jnp.bfloat16)
    grad_y[...] = grad_gated * (gate * gate_sig)
    params_ref[0, 5:6, :] = jnp.sum(branch * gated * inv_gate, 0, keepdims=True)
    params_ref[0, 6:7, :] = jnp.sum(grad_y[...] * mixed_x[...], 0, keepdims=True)
    lane = lax.broadcasted_iota(jnp.int32, (GROUP, 2 * head_size), 1)
    at_last = lax.broadcasted_iota(jnp.int32, (GROUP, 1), 0) == GROUP - 1

    def head_sums(values):
        return (
            jnp.sum(jnp.where(lane < head_size, values, 0.0), 1, keepdims=True),
            jnp.sum(jnp.where(lane < head_size, 0.0, values), 1, keepdims=True),
        )

    grad_state = jnp.zeros((state_width, 2 * head_size), jnp.float32)
    for block in reversed(range(blocks)):
        rows, cum0, cum1, step, tail, enter, keep = block_terms(
            block, cols_ref, masks_ref, head_size
        )
        b_rows, c_rows = bc_ref[rows, :state_width], bc_ref[rows, state_width:]
        x = mixed_x[rows, :]
        dy = grad_y[rows, :]
        x_step = x * step
        score = scores[block]
        decay0 = jnp.exp(jnp.minimum(cum0 - rows_ref[0, 0:1, rows], 0.0))
        decay1 = jnp.exp(jnp.minimum(cum1 - rows_ref[0, 1:2, rows], 0.0))
        dy0 = jnp.where(lane < head_size, dy, 0.0)
        dy1 = jnp.where(lane < head_size, 0.0, dy)
        grad_scores[block] += mm(dy0, x_step, 1, 1) * decay0 + mm(dy1, x_step, 1, 1) * decay1
        inner = mm((score * decay0), dy0, 0, 0) + mm(
            (score * decay1), dy1, 0, 0
        )
        state = states_ref[0, block]
        grad_low = grad_state
        from_state = mm(b_rows, grad_low, 1, 0)
        x_tail = x_step * tail
        grad_bc_ref[rows, :state_width] += mm(x_tail, grad_low, 1, 1)
        grad_xs = inner + from_state * tail
        crossing = from_state * x_tail
        total = jnp.sum(crossing, 0, keepdims=True) + keep * jnp.sum(
            state * grad_state, 0, keepdims=True
        )
        y = ssm_ref[rows, :] - skip_ref[...] * x
        per_token = dy * y - x_step * inner - crossing
        sum0, sum1 = head_sums(jnp.where(at_last, per_token + total, per_token))
        grad_cols_ref[0, rows, 0:1] = sum0
        grad_cols_ref[0, rows, 1:2] = sum1
        step0, step1 = head_sums(grad_xs * x)
        grad_cols_ref[0, rows, 2:3] = step0
        grad_cols_ref[0, rows, 3:4] = step1
        grad_state = grad_state * keep
        if block > 0:
            dy_state = (dy * enter)
            grad_bc_ref[rows, state_width:] += mm(dy_state, state, 1, 1)
            grad_state = grad_state + mm(c_rows, dy_state, 0, 0)
        grad_y[rows, :] = (grad_xs * step + skip_ref[...] * dy) * slope[rows, :]

    grad_conv = grad_y[...]
    stream = value_ref[...]
    masks = masks_ref[...]
    grad_stream = taps_ref[width - 1 : width, :] * grad_conv
    params_ref[0, width - 1 : width, :] = jnp.sum(grad_conv * stream, 0, keepdims=True)
    params_ref[0, 4:5, :] = jnp.sum(grad_conv, 0, keepdims=True)
    params_ref[0, 7:8, :] = jnp.zeros_like(skip_ref)
    for by in range(1, width):
        tap = width - 1 - by
        kept = grad_conv * masks[:, by - 1 : by]
        grad_stream = grad_stream + taps_ref[tap : tap + 1, :] * shifted(kept, -by)
        params_ref[0, tap : tap + 1, :] = jnp.sum(kept * shifted(stream, by), 0, keepdims=True)
    grad_value_ref[...] = grad_stream.astype(jnp.bfloat16)

    @pl.when(pl.program_id(0) == pl.num_programs(0) - 1)
    def _():
        for block in range(blocks):
            rows = pl.ds(block * GROUP, GROUP)
            b_rows, c_rows = bc_ref[rows, :state_width], bc_ref[rows, state_width:]
            kept = keep_pairs(seg_col_ref[rows, :], seg_row_ref[:, rows])
            grad = jnp.where(kept, grad_scores[block], 0.0)
            grad_bc_ref[rows, state_width:] += mm(grad, b_rows, 1, 0)
            grad_bc_ref[rows, :state_width] += mm(grad, c_rows, 0, 0)


def mixer_calls(length, inner, head_size, state_width):
    pairs = inner // (2 * head_size)
    blocks = length // GROUP
    lanes = 2 * head_size
    f32 = jnp.float32
    wide = pl.BlockSpec((length, lanes), lambda i: (0, i))
    states = pl.BlockSpec((1, blocks, state_width, lanes), lambda i: (i, 0, 0, 0))

    def whole(*shape):
        return pl.BlockSpec(shape, lambda i: (0,) * len(shape))

    common = [
        whole(length, 2 * state_width),
        pl.BlockSpec((1, length, 4), lambda i: (i, 0, 0)),
        pl.BlockSpec((1, 2, length), lambda i: (i, 0, 0)),
        whole(length, 8),
        whole(length, 1),
        whole(1, length),
        pl.BlockSpec((4, lanes), lambda i: (0, i)),
        pl.BlockSpec((1, lanes), lambda i: (0, i)),
        pl.BlockSpec((1, lanes), lambda i: (0, i)),
        pl.BlockSpec((1, lanes), lambda i: (0, i)),
    ]
    square = pltpu.VMEM((blocks, GROUP, GROUP), f32)
    column = pltpu.VMEM((length, lanes), f32)
    params = pltpu.CompilerParams(vmem_limit_bytes=VMEM_LIMIT)
    forward = pl.pallas_call(
        lambda *refs: forward_kernel(head_size, *refs),
        grid=(pairs,),
        in_specs=[wide, wide, wide] + common,
        out_specs=(wide, wide, states, whole(length, 2)),
        out_shape=(
            jax.ShapeDtypeStruct((length, inner), f32),
            jax.ShapeDtypeStruct((length, inner), f32),
            jax.ShapeDtypeStruct((pairs, blocks, state_width, lanes), f32),
            jax.ShapeDtypeStruct((length, 2), f32),
        ),
        scratch_shapes=[square, column],
        compiler_params=params,
        name="mixer_forward",
    )
    backward = pl.pallas_call(
        lambda *refs: backward_kernel(head_size, *refs),
        grid=(pairs,),
        in_specs=[wide, wide, wide, wide, states, whole(length, 2)] + common,
        out_specs=(
            wide,
            wide,
            whole(length, 2 * state_width),
            pl.BlockSpec((1, length, 4), lambda i: (i, 0, 0)),
            pl.BlockSpec((1, 8, lanes), lambda i: (i, 0, 0)),
        ),
        out_shape=(
            jax.ShapeDtypeStruct((length, inner), jnp.bfloat16),
            jax.ShapeDtypeStruct((length, inner), jnp.bfloat16),
            jax.ShapeDtypeStruct((length, 2 * state_width), f32),
            jax.ShapeDtypeStruct((pairs, length, 4), f32),
            jax.ShapeDtypeStruct((pairs, 8, lanes), f32),
        ),
        scratch_shapes=[square, square, column, column, column],
        compiler_params=params,
        name="mixer_backward",
    )
    return forward, backward


def local(
    hidden,
    segments,
    norm_gain,
    proj_gate,
    proj_value,
    proj_bc,
    proj_step,
    conv_value,
    conv_bc,
    conv_value_bias,
    conv_bc_bias,
    step_bias,
    decay_log,
    skip_gain,
    gate_gain,
    out_weight,
    cotangent,
):
    seq_count, length = segments.shape
    own_index = lax.axis_index("tensor")
    count = lax.axis_size("dp")
    rows = proj_gate.shape[0]
    inner = proj_gate.shape[1]
    bc_width = proj_bc.shape[1]
    head_count = proj_step.shape[1]
    step_pad = -head_count % 128
    bc_from = 3 * inner
    step_from = bc_from + bc_width
    direct = rows % 16 == 0 and count & (count - 1) == 0
    residual = hidden.astype(jnp.float32)
    inv_rms = lax.rsqrt(jnp.mean(residual * residual, -1, keepdims=True) + EPS)
    normed = (residual * inv_rms * norm_gain[None, :]).astype(jnp.bfloat16)
    bc_pair = both_halves(proj_bc, own_index)
    own_weights = jnp.concatenate(
        [proj_value, proj_gate, out_weight, bc_pair, jnp.pad(proj_step, ((0, 0), (0, step_pad)))], 1
    )
    rows_all = both_halves(normed, own_index)
    cot_all = both_halves(cotangent, own_index)
    if direct:
        weights = gather_rows(own_weights, count)
    else:
        weights = lax.all_gather(own_weights, "dp", axis=0, tiled=True)
    value_full = weights[:, :inner]
    gate_full = weights[:, inner : 2 * inner]
    outw_full = weights[:, 2 * inner : 3 * inner]
    bc_full = weights[:, bc_from:step_from]
    step_full = weights[:, step_from:]
    pre_gate = jnp.dot(rows_all, gate_full, preferred_element_type=jnp.float32)
    pre_value = jnp.dot(rows_all, value_full, preferred_element_type=jnp.float32)
    pre_bc = jnp.dot(rows_all, bc_full, preferred_element_type=jnp.float32)
    pre_step = jnp.dot(rows_all, step_full, preferred_element_type=jnp.float32)[:, :head_count]
    grad_branch = jnp.dot(cot_all, outw_full, preferred_element_type=jnp.float32)
    seg_row = segments.reshape(length)
    blocks = length // GROUP
    head_size = inner // head_count
    pairs = head_count // 2
    forward, backward = mixer_calls(length, inner, head_size, bc_width // 2)

    def mix_bc(stream, taps, offset):
        return jax.nn.silu(conv_mix(stream, taps, offset, seg_row))

    bc_act, pull_bc = jax.vjp(mix_bc, pre_bc, conv_bc, conv_bc_bias)
    shifted_step = pre_step + step_bias[None, :]
    step_rows = jax.nn.softplus(shifted_step)
    decay_rate = -jnp.exp(decay_log)
    triangle = jnp.tril(jnp.ones((GROUP, GROUP), jnp.float32))
    rate_blocks = (step_rows * decay_rate[None, :]).reshape(blocks, GROUP, head_count)
    cum = jnp.einsum("ts,bsh->bth", triangle, rate_blocks, precision=HIGH)
    cum = cum.reshape(length, head_count)
    by_pair = jnp.concatenate(
        [cum.reshape(length, pairs, 2), step_rows.reshape(length, pairs, 2)], 2
    ).transpose(1, 0, 2)
    cum_rows = cum.T.reshape(pairs, 2, length)
    seg_blocks = seg_row.reshape(blocks, GROUP)
    seg_last = seg_blocks[:, GROUP - 1]
    prev_last = jnp.concatenate([jnp.full((1,), -1, jnp.int32), seg_last[:-1]], 0)
    masks = [
        jnp.concatenate([jnp.zeros((by,), bool), seg_row[by:] == seg_row[:-by]], 0)
        for by in range(1, 4)
    ]
    masks += [
        (seg_blocks == prev_last[:, None]).reshape(length),
        (seg_blocks == seg_last[:, None]).reshape(length),
        jnp.broadcast_to((seg_last == prev_last)[:, None], (blocks, GROUP)).reshape(length),
    ]
    masks += [jnp.zeros((length,), bool)] * 2
    common = (
        bc_act,
        by_pair,
        cum_rows,
        jnp.stack(masks, 1).astype(jnp.float32),
        seg_row[:, None],
        seg_row[None, :],
        conv_value,
        conv_value_bias[None, :],
        jnp.repeat(skip_gain, head_size)[None, :],
        gate_gain[None, :],
    )
    gated, ssm_out, states, sums = forward(pre_value, pre_gate, grad_branch, *common)
    sums = (sums.T + swap(sums.T)).T
    inv_gate = lax.rsqrt(sums[:, :1] / DI + EPS)
    pull_scale = inv_gate**3 * (sums[:, 1:] / DI)
    branch_in = (gated * inv_gate * gate_gain[None, :]).astype(jnp.bfloat16)
    branch = own_half(contract_cols(branch_in, outw_full), own_index)
    mixed_out = (residual + branch).astype(jnp.bfloat16)
    grad_out_w = contract_rows(cot_all, branch_in)
    low_gate, low_value, grad_bc_act, grad_cols, params = backward(
        pre_value,
        pre_gate,
        grad_branch,
        ssm_out,
        states,
        jnp.concatenate([inv_gate, pull_scale], 1),
        *common,
    )
    grad_pbc, grad_cbc, grad_cbcb = pull_bc(grad_bc_act)
    grad_cum = grad_cols[:, :, :2].transpose(1, 0, 2).reshape(blocks, GROUP, head_count)
    grad_direct = grad_cols[:, :, 2:].transpose(1, 0, 2).reshape(length, head_count)
    grad_rate = jnp.einsum("ts,bth->bsh", triangle, grad_cum, precision=HIGH)
    grad_rate = grad_rate.reshape(length, head_count)
    grad_ps = (grad_rate * decay_rate[None, :] + grad_direct) * jax.nn.sigmoid(shifted_step)
    grad_sb = jnp.sum(grad_ps, 0)
    grad_dl = jnp.sum(grad_rate * step_rows, 0) * decay_rate
    by_channel = params.transpose(1, 0, 2).reshape(8, inner)
    grad_cv = by_channel[:4]
    grad_cvb = by_channel[4]
    grad_gate_gain = by_channel[5]
    grad_sk = jnp.sum(by_channel[6].reshape(head_count, head_size), 1)
    low_step = jnp.pad(grad_ps, ((0, 0), (0, step_pad))).astype(jnp.bfloat16)
    grad_rows = contract_cols(low_gate, gate_full) + contract_cols(low_value, value_full)
    grad_rows = grad_rows + contract_cols(low_step, step_full)
    grad_rows_own = own_half(grad_rows, own_index)
    low_bc = own_half(grad_pbc, own_index).astype(jnp.bfloat16)
    grad_normed = grad_rows_own + contract_cols(low_bc, bc_full)
    weighted_in = grad_normed * norm_gain[None, :]
    grad_norm_part = jnp.sum(grad_normed * residual * inv_rms, 0)
    grad_input = (
        cotangent.astype(jnp.float32)
        + inv_rms * weighted_in
        - residual * inv_rms**3 * jnp.sum(weighted_in * residual, -1, keepdims=True) / D
    )
    parts = jnp.concatenate(
        [
            contract_rows(rows_all, low_value),
            contract_rows(rows_all, low_gate),
            grad_out_w,
            contract_rows(normed, low_bc),
            contract_rows(rows_all, low_step),
        ],
        1,
    )

    def as_row(values):
        flat = values.reshape(1, -1)
        return jnp.pad(flat, ((0, 0), (0, inner - flat.shape[1])))

    bc_rows = -(-4 * bc_width // inner)
    small = jnp.concatenate(
        [
            grad_cv,
            as_row(grad_cvb),
            as_row(grad_gate_gain),
            as_row(jnp.concatenate([grad_sb, grad_dl, grad_sk])),
            as_row(grad_norm_part[:0]),
            as_row(grad_norm_part),
            as_row(grad_cbcb),
            jnp.pad(grad_cbc.reshape(-1), (0, bc_rows * inner - 4 * bc_width)).reshape(bc_rows, inner),
            jnp.zeros((6 - bc_rows, inner), jnp.float32),
        ],
        0,
    )
    if direct:
        gw, gw_bc, small = scatter_rows(parts.astype(jnp.bfloat16), small, count, bc_from, bc_width)
    else:
        gw = lax.psum_scatter(parts, "dp", scatter_dimension=0, tiled=True)
        gw_bc = lax.psum_scatter(
            gw[:, bc_from:step_from], "tensor", scatter_dimension=0, tiled=True
        )
        small = lax.psum(small, "dp")
        small = jnp.concatenate([small[:8], lax.psum(small[8:], "tensor")], 0)
    heads = small[6]
    return (
        mixed_out,
        grad_input,
        small[8],
        gw[:, inner : 2 * inner],
        gw[:, :inner],
        gw_bc,
        gw[:, step_from : step_from + head_count],
        small[:4],
        small[10 : 10 + bc_rows].reshape(-1)[: 4 * bc_width].reshape(4, bc_width),
        small[4],
        small[9, :bc_width],
        heads[:head_count],
        heads[head_count : 2 * head_count],
        heads[2 * head_count : 3 * head_count],
        small[5],
        gw[:, 2 * inner : 3 * inner],
    )


def solution(mesh):
    in_specs = (
        P(("dp", "tensor"), None),
        P("dp", None),
        P(),
        P("dp", "tensor"),
        P("dp", "tensor"),
        P(("dp", "tensor"), None),
        P("dp", "tensor"),
        P(None, "tensor"),
        P(),
        P("tensor"),
        P(),
        P("tensor"),
        P("tensor"),
        P("tensor"),
        P("tensor"),
        P("dp", "tensor"),
        P(("dp", "tensor"), None),
    )
    out_specs = (
        P(("dp", "tensor"), None),
        P(("dp", "tensor"), None),
        P(),
        P("dp", "tensor"),
        P("dp", "tensor"),
        P(("dp", "tensor"), None),
        P("dp", "tensor"),
        P(None, "tensor"),
        P(),
        P("tensor"),
        P(),
        P("tensor"),
        P("tensor"),
        P("tensor"),
        P("tensor"),
        P("dp", "tensor"),
    )
    return jax.shard_map(local, mesh=mesh, in_specs=in_specs, out_specs=out_specs, check_vma=False)
```
